32 devices in a mesh: mp: 2 (over x), row: 4 (over z), col: 4 (over y, core).
Axes of the slice: x: 2, y: 2, z: 4, core: 2. Of those that a mesh axis runs over, the one named last changes fastest.
Arguments:
- gram_tiles: bfloat16 [4, 4, 4, 1024, 16384], P('mp', None, 'row', None, 'col'), may hold values from -4 to 64, as said below
- weights: bfloat16 [4, 16384, 128], P('mp', ('col', 'row')), may hold values from -8 to 8
- damping: float32 [128], replicated, may hold values from 0.5 to 4
Outputs:
- merged: float32 [16384, 128], P(('col', 'row'))
- residual: float32 [16384, 128], P(('col', 'row'))
The draws below stay inside these ranges and needn't reach their ends.
Inputs may be any that keep to these rules, and one draw needn't show every extreme that they name: `gram_tiles`: each model's 16384 x 16384 Gram, read as in the first step, is symmetric positive definite.
All inputs are finite; a program needn't handle non-finite values.
Results may differ from the reference program's by a relative error of at most 0.012.
The reference program's roundings to bfloat16 on the way count: a program that leaves them out, or rounds other values in their place, can miss the bound.
Values may be sent and summed in bfloat16 or wider, within the bound.
A program may use at most 128 MiB of HBM per device.

```python
import math
import jax
import jax.numpy as jnp
from jax import lax

D = 16384
K = 128
ITERS = 2
MODELS = 4
ROW_BLOCKS = 4
COL_BLOCKS = 4
PIECE = 1024


def draw_gram_tiles(key, part):
    model_keys = jax.random.split(jax.random.fold_in(key, 11), MODELS)
    block_key = jax.random.fold_in(key, 31)
    order = jax.random.permutation(block_key, ROW_BLOCKS).astype(jnp.float32)
    exponent = -0.5 + order / float(max(ROW_BLOCKS - 1, 1))
    block_values = jnp.exp(exponent * math.log(3.0))
    block_of = jnp.arange(D) // PIECE % ROW_BLOCKS
    block_scale = block_values[block_of]

    def one_model(model_key):
        first_key, second_key = jax.random.split(model_key, 2)
        normal_part = jax.random.truncated_normal(first_key, -4.0, 4.0, (D, D), jnp.float32)
        symmetric = (normal_part + normal_part.T) * (1.0 / math.sqrt(2.0 * D))
        diagonal = jax.random.uniform(second_key, (D,), jnp.float32, 2.5, 6.0)
        positions = jnp.arange(D)
        symmetric = symmetric.at[positions, positions].add(diagonal)
        scales = block_scale
        symmetric = symmetric * scales[:, None] * scales[None, :]
        return symmetric.astype(jnp.bfloat16)
    grams = lax.map(one_model, model_keys)
    return grams.reshape(MODELS, COL_BLOCKS, ROW_BLOCKS, PIECE, D)


def draw_weights(key, part):
    first_key = jax.random.fold_in(jax.random.fold_in(key, 23), 0)
    row_scale = 0.6 + 1.2 * jnp.arange(D, dtype=jnp.float32) / (D - 1)
    values = jax.random.truncated_normal(first_key, -4.0, 4.0, (MODELS, D, K), jnp.float32)
    return (values * row_scale[None, :, None]).astype(jnp.bfloat16)


def setup_inputs(seed: int = 0) -> dict:
    keys = jax.random.split(jax.random.key(seed), 4)
    return {
        "gram_tiles": draw_gram_tiles(jax.random.fold_in(keys[3], 71), 0),
        "weights": draw_weights(jax.random.fold_in(keys[3], 71), 0),
        "damping": jnp.clip(jnp.exp(jax.random.uniform(keys[2], (K,), jnp.float32, math.log(0.5), math.log(4.0))), 0.5, 4.0),
    }


def apply_models(matrices, vectors):
    def add_model(running, operands):
        matrix, vector = operands
        return running + jnp.dot(matrix, vector, preferred_element_type=jnp.float32), None

    initial = jnp.zeros((D, K), jnp.float32)
    running, unused = lax.scan(add_model, initial, (matrices, vectors))
    return running


def reference(gram_tiles, weights, damping):
    matrices = gram_tiles.reshape(MODELS, D, D)
    target = apply_models(matrices, weights)
    merged = jnp.zeros((D, K), jnp.float32)
    residual = target
    direction = target
    norm_now = jnp.sum(residual * residual, axis=0)
    for iteration in range(ITERS):
        low_dir = direction.astype(jnp.bfloat16)
        applied = apply_models(matrices, jnp.broadcast_to(low_dir[None], (MODELS, D, K)))
        dir_wide = low_dir.astype(jnp.float32)
        applied = applied + damping[None, :] * dir_wide
        curve_term = jnp.sum(dir_wide * applied, axis=0)
        step_size = norm_now / curve_term
        merged = merged + step_size[None, :] * direction
        residual = residual - step_size[None, :] * applied
        if iteration + 1 < ITERS:
            norm_next = jnp.sum(residual * residual, axis=0)
            direction = residual + (norm_next / norm_now)[None, :] * direction
            norm_now = norm_next
    return merged, residual
```

```python
import functools

import jax
import jax.numpy as jnp
from jax import lax
from jax.experimental import pallas as pl
from jax.experimental.pallas import tpu as pltpu
from jax.sharding import PartitionSpec as P

ITERS = 2
NBUF = 8
MESH = pl.DeviceIdType.MESH
F32 = jnp.float32
BF16 = jnp.bfloat16


def kernel(n_mp, n_row, n_col, gram, w_ref, damp, merged, resid,
           gsum, stage, part, xg, lg, csend, crecv, ysend, yrecv, mwide, mbuf, diag, dirn, sc1, sc2,
           gsem, zs, zr, xs, xr, cs, cr, ys, yr, ms, mr, ds, dr, s1s, s1r, s2s, s2r):
    M, R, C = n_mp, n_row, n_col
    H = C // 2
    models, piece, width = w_ref.shape
    half = piece // M
    tile = min(piece, 256)
    parts = piece // tile
    mp, r, c = lax.axis_index("mp"), lax.axis_index("row"), lax.axis_index("col")
    h, core = c // 2, c % 2

    def at_row(k):
        return {"row": k}

    def at_col(k):
        return {"col": k}

    def at_mp(k):
        return {"mp": k}

    def remote(src, dst, send, recv, device):
        return pltpu.make_async_remote_copy(
            src_ref=src, dst_ref=dst, send_sem=send, recv_sem=recv,
            device_id=device, device_id_type=MESH)

    def piece_at(i):
        low = jnp.minimum(r, R - 1 - r)
        d = (i + 1) // 2
        both = jnp.where(i % 2 == 1, r - d, r + d)
        one = jnp.where(r < R - 1 - r, r + (i - low), r - (i - low))
        return jnp.where(i <= 2 * low, both, one)

    def col_at(k):
        group = (h + k // 2 + 1) % H
        return 2 * group + jnp.where(k % 2 == 0, 1 - core, core)

    def stream(u):
        t = u // parts
        p, cc = piece_at(t // C), col_at(t % C)
        slot = u % NBUF
        return pltpu.make_async_copy(
            gram.at[:, cc, rows_of(u % parts), pl.ds(pl.multiple_of(p * piece, piece), piece)],
            stage.at[slot], gsem.at[slot])

    def rows_of(j):
        return pl.ds(pl.multiple_of(j * tile, tile), tile)

    for u in range(min(NBUF - 1, R * C * parts)):
        stream(u).start()

    barrier = pltpu.get_barrier_semaphore()
    for k in range(1, C):
        pl.semaphore_signal(barrier, inc=1, device_id=at_col((c + k) % C), device_id_type=MESH)
    for k in range(1, R):
        pl.semaphore_signal(barrier, inc=1, device_id=at_row((r + k) % R), device_id_type=MESH)
    for k in range(1, M):
        pl.semaphore_signal(barrier, inc=1, device_id=at_mp((mp + k) % M), device_id_type=MESH)
    pl.semaphore_wait(barrier, C + R + M - 3)

    def zref(n, p):
        if n == 0:
            return xg.at[p]
        return lg.at[n - 1, p, pl.ds(pl.multiple_of(mp * half, half), half)]

    def zcopy(n, p, up):
        ref = zref(n, p)
        return remote(ref, ref, zs.at[n, up, p], zr.at[n, p], at_row(r + 1 if up else r - 1))

    def zsend(n, p, wait=False):
        @pl.when(jnp.logical_and(p <= r, r < R - 1))
        def _():
            copy = zcopy(n, p, 1)
            copy.wait_send() if wait else copy.start()

        @pl.when(jnp.logical_and(p >= r, r > 0))
        def _():
            copy = zcopy(n, p, 0)
            copy.wait_send() if wait else copy.start()

    def zwait(n, p):
        ref = zref(n, p)
        remote(ref, ref, zs.at[n, 0, p], zr.at[n, p],
               at_row(jnp.where(p < r, r - 1, r + 1))).wait_recv()

    def xcopy(n, p, k):
        ref = lg.at[n - 1, p, pl.ds(pl.multiple_of(mp * half, half), half)]
        return remote(ref, ref, xs.at[n, k - 1, p], xr.at[n, k - 1, p], at_mp((mp + k) % M))

    def xwait(n, p, k):
        other = (mp + M - k) % M
        ref = lg.at[n - 1, p, pl.ds(pl.multiple_of(other * half, half), half)]
        remote(ref, ref, xs.at[n, k - 1, p], xr.at[n, k - 1, p], at_mp(other)).wait_recv()

    def first_block(t, p):
        cc = col_at(t % C)

        def body(j, carry):
            u = t * parts + j
            stream(u).wait()

            @pl.when(u + NBUF - 1 < R * C * parts)
            def _():
                stream(u + NBUF - 1).start()

            slot = u % NBUF
            rows = rows_of(j)
            value = part[cc, rows, :]
            total = None
            for m in range(models):
                g = stage[slot, m]
                value += jnp.dot(g, xg[p, m], preferred_element_type=F32)
                total = g if total is None else total + g
            part[cc, rows, :] = value
            gsum[cc, p, rows, :] = total

            if not isinstance(t, int) or t == C - 1:
                @pl.when(t == C - 1)
                def _():
                    split_diagonal(j, slot)

            return carry

        lax.fori_loop(0, parts, body, 0)

    def diag_copy(m, k, device):
        return remote(diag.at[m], diag.at[m], ds.at[k - 1], dr.at[k - 1], at_mp(device))

    def split_diagonal(j, slot):
        rows = rows_of(j)
        wide = None
        for m in range(models):
            g = stage[slot, m].astype(F32)
            wide = g if wide is None else wide + g
        row_ids = lax.broadcasted_iota(jnp.int32, (tile, piece), 0) + j * tile
        on = row_ids == lax.broadcasted_iota(jnp.int32, (tile, piece), 1)
        gsum[c, r, rows, :] = jnp.where(on, 0.0, wide).astype(BF16)
        column = jnp.sum(jnp.where(on, wide, 0.0), axis=1, keepdims=True)
        diag[mp, rows, :] = jnp.broadcast_to(column, (tile, width))

    def later_block(n, cc, p):
        def body(j, carry):
            rows = rows_of(j)
            part[cc, rows, :] += jnp.dot(
                gsum[cc, p, rows, :], lg[n - 1, p], preferred_element_type=F32)
            return carry

        lax.fori_loop(0, piece // tile, body, 0)

    def finish(n, block):
        def core_copy(s):
            return remote(csend.at[s], crecv.at[n, s], cs.at[n, s], cr.at[n, s], at_col(c + 1 - 2 * core))

        def y_copy(s):
            return remote(ysend.at[s], yrecv.at[n, s], ys.at[n, s], yr.at[n, s],
                          at_col(2 * ((h + s + 1) % H) + core))

        for s in range(H):
            group = (h + s + 1) % H
            theirs, mine = 2 * group + 1 - core, 2 * group + core
            block(2 * s, theirs)
            csend[s] = part[theirs].astype(BF16)
            core_copy(s).start()
            block(2 * s + 1, mine)
            core_copy(s).wait_recv()
            value = part[mine] + crecv[n, s].astype(F32)
            if s < H - 1:
                ysend[s] = value.astype(BF16)
                y_copy(s).start()
        for s in range(H - 1):
            y_copy(s).wait_recv()
            value += yrecv[n, s].astype(F32)
        held = mwide if n == 0 else mbuf.at[n - 1]

        def m_copy(m, k, device):
            return remote(held.at[m], held.at[m], ms.at[n, k - 1], mr.at[n, k - 1], at_mp(device))

        held[mp] = value.astype(held.dtype)
        for k in range(1, M):
            m_copy(mp, k, (mp + k) % M).start()
        for k in range(1, M):
            other = (mp + M - k) % M
            m_copy(other, k, other).wait_recv()
        total = held[0].astype(F32)
        for m in range(1, M):
            total += held[m].astype(F32)
        for s in range(H):
            core_copy(s).wait_send()
            if s < H - 1:
                y_copy(s).wait_send()
        for k in range(1, M):
            m_copy(mp, k, (mp + k) % M).wait_send()
        return total

    def drain(n):
        for p in range(R):
            zsend(n, p, wait=True)
            if n > 0:
                @pl.when(p != r)
                def _():
                    for k in range(1, M):
                        xcopy(n, p, k).wait_send()

    def first_pass():
        xg[r] = w_ref[...]
        zsend(0, r)
        part[...] = jnp.zeros_like(part)

        def outer(i, carry):
            p = piece_at(i)

            @pl.when(i > 0)
            def _():
                zwait(0, p)
                zsend(0, p)

            def inner(k, carry):
                first_block(i * C + k, p)
                return carry

            lax.fori_loop(0, C, inner, carry)

            @pl.when(i == 0)
            def _():
                for k in range(1, M):
                    diag_copy(mp, k, (mp + k) % M).start()

            return carry

        lax.fori_loop(0, R - 1, outer, 0)
        last = piece_at(R - 1)
        if R > 1:
            zwait(0, last)
            zsend(0, last)
        total = finish(0, lambda k, cc: first_block((R - 1) * C + k, last))
        drain(0)
        for k in range(1, M):
            other = (mp + M - k) % M
            diag_copy(other, k, other).wait_recv()
            diag_copy(mp, k, (mp + k) % M).wait_send()
        return total

    def later_pass(n):
        zsend(n, r)
        part[...] = jnp.zeros_like(part)

        def ready(p):
            for k in range(1, M):
                xwait(n, p, k)

        def outer(i, carry):
            p = piece_at(i)
            zwait(n, p)
            zsend(n, p)
            for k in range(1, M):
                xcopy(n, p, k).start()
            before = piece_at(i - 1)

            @pl.when(i > 1)
            def _():
                ready(before)

            def inner(cc, carry):
                later_block(n, cc, before)
                return carry

            return lax.fori_loop(0, C, inner, carry)

        lax.fori_loop(1, R, outer, 0)
        last = piece_at(R - 1)
        if R > 1:
            ready(last)
        total = finish(n, lambda k, cc: later_block(n, cc, last))
        drain(n)
        return total

    def reduce_small(it, value):
        sc1[it, c] = value
        for k in range(1, C):
            remote(sc1.at[it, c], sc1.at[it, c], s1s.at[it, k - 1], s1r.at[it, k - 1],
                   at_col((c + k) % C)).start()
        for k in range(1, C):
            other = (c + C - k) % C
            remote(sc1.at[it, other], sc1.at[it, other], s1s.at[it, k - 1], s1r.at[it, k - 1],
                   at_col(other)).wait_recv()
        sc2[it, r] = jnp.sum(sc1[it], axis=0)
        for k in range(1, R):
            remote(sc2.at[it, r], sc2.at[it, r], s2s.at[it, k - 1], s2r.at[it, k - 1],
                   at_row((r + k) % R)).start()
        for k in range(1, R):
            other = (r + R - k) % R
            remote(sc2.at[it, other], sc2.at[it, other], s2s.at[it, k - 1], s2r.at[it, k - 1],
                   at_row(other)).wait_recv()
        total = jnp.sum(sc2[it], axis=0)
        for k in range(1, C):
            remote(sc1.at[it, c], sc1.at[it, c], s1s.at[it, k - 1], s1r.at[it, k - 1],
                   at_col((c + k) % C)).wait_send()
        for k in range(1, R):
            remote(sc2.at[it, r], sc2.at[it, r], s2s.at[it, k - 1], s2r.at[it, k - 1],
                   at_row((r + k) % R)).wait_send()
        return total

    def dots(*pairs):
        sums = [jnp.sum(a * b, axis=0, keepdims=True) for a, b in pairs]
        sums.append(jnp.zeros((8 - len(pairs), width), F32))
        return jnp.concatenate(sums, axis=0)

    target = first_pass()
    resid[...] = target
    dirn[...] = target
    lg[0, r] = target.astype(BF16)
    norm_now = None
    for it in range(ITERS):
        applied = later_pass(it + 1)
        wide = lg[it, r].astype(F32)
        scale = damp[...] + diag[0]
        for m in range(1, n_mp):
            scale += diag[m]
        applied = applied + scale * wide
        old = resid[...]
        if it + 1 < ITERS:
            pairs = [(wide, applied), (old, applied), (applied, applied)]
            if norm_now is None:
                pairs.append((old, old))
            sums = reduce_small(it, dots(*pairs))
            if norm_now is None:
                norm_now = sums[3:4]
        else:
            sums = reduce_small(it, dots((wide, applied)))
        step = norm_now / sums[0:1]
        direction = dirn[...]
        if it == 0:
            merged[...] = step * direction
        else:
            merged[...] += step * direction
        new = old - step * applied
        resid[...] = new
        if it + 1 < ITERS:
            norm_next = norm_now + step * (step * sums[2:3] - 2.0 * sums[1:2])
            direction = new + (norm_next / norm_now) * direction
            dirn[...] = direction
            lg[it + 1, r] = direction.astype(BF16)
            norm_now = norm_next


def solution(mesh):
    n_mp, n_row, n_col = mesh.shape["mp"], mesh.shape["row"], mesh.shape["col"]

    def on_device(gram_tiles, weights, damping):
        shape = gram_tiles.shape
        models, piece, width = shape[0], weights.shape[1], weights.shape[2]
        passes, groups = ITERS + 1, n_col // 2
        gram = gram_tiles.reshape(models, shape[1], shape[3], shape[4])
        dma = pltpu.SemaphoreType.DMA
        vmem = pl.BlockSpec(memory_space=pltpu.VMEM)
        out = jax.ShapeDtypeStruct((piece, width), F32)
        return pl.pallas_call(
            functools.partial(kernel, n_mp, n_row, n_col),
            out_shape=(out, out),
            in_specs=[pl.BlockSpec(memory_space=pl.ANY), vmem, vmem],
            out_specs=(vmem, vmem),
            scratch_shapes=[
                pltpu.VMEM((n_col, n_row, piece, piece), BF16),
                pltpu.VMEM((NBUF, models, min(piece, 256), piece), BF16),
                pltpu.VMEM((n_col, piece, width), F32),
                pltpu.VMEM((n_row, models, piece, width), BF16),
                pltpu.VMEM((ITERS, n_row, piece, width), BF16),
                pltpu.VMEM((groups, piece, width), BF16),
                pltpu.VMEM((passes, groups, piece, width), BF16),
                pltpu.VMEM((groups, piece, width), BF16),
                pltpu.VMEM((passes, groups, piece, width), BF16),
                pltpu.VMEM((n_mp, piece, width), F32),
                pltpu.VMEM((ITERS, n_mp, piece, width), BF16),
                pltpu.VMEM((n_mp, piece, width), F32),
                pltpu.VMEM((piece, width), F32),
                pltpu.VMEM((ITERS, n_col, 8, width), F32),
                pltpu.VMEM((ITERS, n_row, 8, width), F32),
                dma((NBUF,)),
                dma((passes, 2, n_row)),
                dma((passes, n_row)),
                dma((passes, n_mp, n_row)),
                dma((passes, n_mp, n_row)),
                dma((passes, groups)),
                dma((passes, groups)),
                dma((passes, groups)),
                dma((passes, groups)),
                dma((passes, n_mp)),
                dma((passes, n_mp)),
                dma((n_mp,)),
                dma((n_mp,)),
                dma((ITERS, n_col)),
                dma((ITERS, n_col)),
                dma((ITERS, n_row)),
                dma((ITERS, n_row)),
            ],
            compiler_params=pltpu.CompilerParams(
                collective_id=0, has_side_effects=True, vmem_limit_bytes=62 * 1024 * 1024),
        )(gram, weights, damping.reshape(1, width))

    in_specs = (P("mp", None, "row", None, "col"), P("mp", ("col", "row"), None), P())
    out_specs = (P(("col", "row"), None), P(("col", "row"), None))
    return jax.shard_map(
        on_device, mesh=mesh, in_specs=in_specs, out_specs=out_specs, check_vma=False
    )
```
